256 devices in a mesh: ctx: 32 (over y, x, core), head: 8 (over z).
Axes of the slice: x: 4, y: 4, z: 8, core: 2. Of those that a mesh axis runs over, the one named last changes fastest.
Arguments:
- queries: bfloat16 [8192, 4096], P(('ctx', 'head')), may hold values from -0.59765625 to 0.59765625
- key_in: bfloat16 [8192, 4096], P(('ctx', 'head')), may hold values from -0.59765625 to 0.59765625
- values_in: bfloat16 [8192, 4096], P(('ctx', 'head')), may hold values from -6 to 6
- strength: bfloat16 [8192, 32], P(('ctx', 'head')), may hold values from 0 to 0.95, as said below
- log_decay: bfloat16 [8192, 4096], P(('ctx', 'head')), may hold values from -1.2 to 0, as said below
- d_out: bfloat16 [8192, 4096], P(('ctx', 'head')), may hold values from -6 to 6
Outputs:
- d_queries: bfloat16 [8192, 4096], P(('ctx', 'head'))
- d_keys: bfloat16 [8192, 4096], P(('ctx', 'head'))
- d_values: bfloat16 [8192, 4096], P(('ctx', 'head'))
- d_strength: bfloat16 [8192, 32], P(('ctx', 'head'))
- d_log_decay: bfloat16 [8192, 4096], P(('ctx', 'head'))
The draws below stay inside these ranges and needn't reach their ends.
Inputs may be any that keep to these rules, and one draw needn't show every extreme that they name: `log_decay`: every log decay is negative. Every write strength is positive and below one.
All inputs are finite; a program needn't handle non-finite values.
Results may differ from the reference program's by a relative error of at most 0.00215.
Values may be sent and summed in bfloat16 or wider, within the bound.
No kernel may reach another device: no remote copies, remote signals or barrier semaphores. Data moves between devices by JAX's collectives and lax.ppermute only.
A program may use at most 128 MiB of HBM per device.

```python
import jax
import jax.numpy as jnp
from jax import lax

HEADS = 32
HEAD_DIM = 128
SPAN = 64
TOK_CTX = 256
TOKENS = 8192


def draw_strength(key, part):
    shards = TOKENS // TOK_CTX
    pick_key, strong_key, weak_key, block_key, rough_key = jax.random.split(key, 5)
    share = 3
    strong_head = jax.random.randint(pick_key, (HEADS,), 0, 8) < share
    strong_value = jax.random.uniform(strong_key, (TOKENS, HEADS), jnp.float32, 0.2, 0.95)
    weak_base = jnp.exp(jax.random.uniform(weak_key, (HEADS,), jnp.float32, jnp.log(0.1), jnp.log(1.5))) * (HEAD_DIM / TOKENS)
    block_factor = jnp.exp(jax.random.uniform(block_key, (shards, 1, HEADS), jnp.float32, -0.7, 0.7))
    rough_factor = jnp.exp(jax.random.uniform(rough_key, (shards, TOK_CTX, HEADS), jnp.float32, -0.7, 0.7))
    weak_value = jnp.minimum((weak_base * block_factor * rough_factor).reshape(TOKENS, HEADS), 0.95)
    return jnp.where(strong_head[None, :], strong_value, weak_value).astype(jnp.bfloat16)


def draw_log_decay(key, part):
    channels = HEADS * HEAD_DIM
    shards = TOKENS // TOK_CTX
    pick_key, fast_key, slow_key, block_key, rough_key, spot_key, cut_key = jax.random.split(key, 7)
    share = 4
    fast_mask = jax.random.randint(pick_key, (channels,), 0, 8) < share
    fast_rate = jnp.exp(jax.random.uniform(fast_key, (channels,), jnp.float32, jnp.log(0.06), jnp.log(0.1)))
    slow_rate = jax.random.uniform(slow_key, (channels,), jnp.float32, 0.1, 1.0) * (1.0 / TOKENS)
    base_rate = jnp.where(fast_mask, fast_rate, slow_rate)
    block_factor = jnp.exp(jax.random.uniform(block_key, (shards, 1, channels), jnp.float32, -0.7, 0.7))
    rough_factor = jnp.exp(jax.random.uniform(rough_key, (shards, TOK_CTX, channels), jnp.float32, -0.7, 0.7))
    rates = (base_rate * block_factor * rough_factor).reshape(TOKENS, channels)
    spots = jax.random.randint(spot_key, (3,), 0, TOKENS)
    struck = jnp.any(jnp.arange(TOKENS)[:, None] == spots[None, :], axis=1)
    cuts = jnp.log(jax.random.uniform(cut_key, (TOKENS, channels), jnp.float32, 0.5, 0.8))
    return (jnp.where(struck[:, None], cuts, 0.0) - rates).astype(jnp.bfloat16)


def block_scale(rng, dims, cuts, least, top_value):
    def one(position, blocks):
        steps = jax.random.uniform(jax.random.fold_in(jax.random.fold_in(rng, 6), position), (blocks,), jnp.float32, least / len(cuts), top_value / len(cuts))
        return jnp.repeat(jnp.exp(steps), dims[position] // blocks).reshape((-1,) + (1,) * (len(dims) - position - 1))

    factor_of = one(*cuts[0])
    for cut in cuts[1:]:
        factor_of = factor_of * one(*cut)
    return factor_of


def gaussian(key, shape, width, bound, cuts=(), held_as=jnp.bfloat16):
    loudness = block_scale(key, shape, cuts, -0.22, 0.18) if cuts else 1.0
    values = jax.random.normal(key, shape, jnp.float32) * width * loudness
    return jnp.minimum(jnp.maximum(values, -bound), bound).astype(held_as)


def setup_inputs(seed: int = 0) -> dict:
    splits = jax.random.split(jax.random.key(seed), 7)
    queries = gaussian(splits[0], (TOKENS, HEADS * HEAD_DIM), 0.088, 0.59765625, ((0, 256),))
    key_in = gaussian(splits[1], (TOKENS, HEADS * HEAD_DIM), 0.088, 0.59765625, ((0, 256),))
    values_in = gaussian(splits[2], (TOKENS, HEADS * HEAD_DIM), 1.0, 6.0, ((0, 256),))
    strength = draw_strength(jax.random.fold_in(splits[6], 71), 0)
    log_decay = draw_log_decay(jax.random.fold_in(splits[6], 71), 0)
    d_out = gaussian(splits[5], (TOKENS, HEADS * HEAD_DIM), 1.0, 6.0, ((0, 256),))
    return {"queries": queries, "key_in": key_in, "values_in": values_in, "strength": strength, "log_decay": log_decay, "d_out": d_out}


exact_prec = lax.Precision.HIGHEST
epsilon = 1e-06

def prepare(queries, keys_used, values_used, strength, log_decay):
    span_len = queries.shape[1]
    head_width = queries.shape[3]
    q_unit = queries * lax.rsqrt(lax.optimization_barrier(jnp.sum(queries * queries, axis=3, keepdims=True)) + epsilon) * head_width ** (-0.5)
    k_unit = keys_used * lax.rsqrt(lax.optimization_barrier(jnp.sum(keys_used * keys_used, axis=3, keepdims=True)) + epsilon)
    gamma = jnp.cumsum(log_decay, axis=1)
    middle = gamma[:, span_len // 2 - 1:span_len // 2]
    q_rise = q_unit * jnp.exp(gamma - middle)
    k_rise = k_unit * jnp.exp(gamma - middle)
    k_fall = k_unit * jnp.exp(middle - gamma)
    strict_mask = jnp.tril(jnp.ones((span_len, span_len), jnp.float32), -1)
    causal_mask = jnp.tril(jnp.ones((span_len, span_len), jnp.float32))
    key_inner = jnp.einsum('ntha,nsha->nhts', k_rise, k_fall, precision=exact_prec) * strict_mask
    scores = jnp.einsum('ntha,nsha->nhts', q_rise, k_fall, precision=exact_prec) * causal_mask
    strength_t = jnp.transpose(strength, (0, 2, 1))
    system = jnp.eye(span_len, dtype=jnp.float32) + strength_t[..., None] * key_inner
    k_head = k_unit * jnp.exp(gamma)
    right_side = jnp.concatenate([values_used, k_head], axis=3) * strength[..., None]
    right_side = jnp.transpose(right_side, (0, 2, 1, 3))
    solved = lax.linalg.triangular_solve(system, right_side, left_side=True, lower=True, unit_diagonal=True)
    w_value = solved[..., :head_width]
    w_key = solved[..., head_width:]
    gamma_end = gamma[:, -1:]
    key_tail = k_unit * jnp.exp(gamma_end - gamma)
    fade_last = jnp.exp(gamma_end[:, 0])
    q_head = q_unit * jnp.exp(gamma)
    return (q_head, scores, w_value, w_key, key_tail, fade_last)

def march(w_value, w_key, key_tail, fade_last, state):

    def advance(state_now, piece_data):
        value_part, key_part, tail_part, fade_part = piece_data
        updates = value_part - jnp.einsum('hta,hab->htb', key_part, state_now, precision=exact_prec)
        following = fade_part[:, :, None] * state_now + jnp.einsum('tha,htb->hab', tail_part, updates, precision=exact_prec)
        return (following, (state_now, updates))
    final_state, (start_states, all_updates) = lax.scan(advance, state, (w_value, w_key, key_tail, fade_last))
    return (final_state, start_states, all_updates)

def sweep(prepared, state):
    q_head, scores, w_value, w_key, key_tail, fade_last = prepared
    final_state, start_states, all_updates = march(w_value, w_key, key_tail, fade_last, state)
    output = jnp.einsum('ntha,nhab->nthb', q_head, start_states, precision=exact_prec)
    output = output + jnp.einsum('nhts,nhsb->nthb', scores, all_updates, precision=exact_prec)
    return (output, final_state)

def reference(queries, key_in, values_in, strength, log_decay, d_out):
    heads_all = strength.shape[1]
    head_width = queries.shape[1] // heads_all
    total = queries.shape[0]
    blocks = total // SPAN

    def by_head(array):
        return jnp.transpose(array.reshape(total, heads_all, head_width), (1, 0, 2))

    def one_head(packed):
        q_one, k_one, v_one, s_one, g_one, o_one = packed

        def shaped(array):
            return array.astype(jnp.float32).reshape(blocks, SPAN, 1, head_width)

        def forward(q_in, k_in, v_in, s_in, g_in):
            prepared = prepare(q_in, k_in, v_in, s_in, g_in)
            return sweep(prepared, jnp.zeros((1, head_width, head_width), jnp.float32))[0]
        strength_one = s_one.astype(jnp.float32).reshape(blocks, SPAN, 1)
        _, pull = jax.vjp(forward, shaped(q_one), shaped(k_one), shaped(v_one), strength_one, shaped(g_one))
        d_q, d_k, d_v, d_s, d_g = pull(shaped(o_one))

        def flatten(array):
            return array.reshape(total, head_width).astype(jnp.bfloat16)
        return (flatten(d_q), flatten(d_k), flatten(d_v), d_s.reshape(total).astype(jnp.bfloat16), flatten(d_g))
    results = lax.map(one_head, (by_head(queries), by_head(key_in), by_head(values_in), jnp.transpose(strength), by_head(log_decay), by_head(d_out)))

    def regather(array):
        return jnp.transpose(array, (1, 0, 2)).reshape(total, heads_all * head_width)
    return (regather(results[0]), regather(results[1]), regather(results[2]), jnp.transpose(results[3]), regather(results[4]))
```

```python
import jax
import jax.numpy as jnp
from jax import lax
from jax.experimental import pallas as pl
from jax.experimental.pallas import tpu as pltpu
from jax.sharding import Mesh, PartitionSpec as P

epsilon = 1e-06
bf16 = jnp.bfloat16
f32 = jnp.float32
CHUNK = 128
VMEM_BYTES = 56 << 20


def params():
    return pltpu.CompilerParams(vmem_limit_bytes=VMEM_BYTES)


def parts(value):
    high = value.astype(bf16)
    return (high, (value - high.astype(f32)).astype(bf16))


def beside(arrays, axis):
    return arrays[0] if len(arrays) == 1 else jnp.concatenate(arrays, axis)


def product(left, right, left_axis=1, right_axis=0):
    wide = right[0].shape[1 - right_axis]
    row = beside(right, 1 - right_axis)
    stacked = beside([row] * len(left), right_axis)
    lengthened = beside(left, left_axis)
    found = lax.dot_general(
        lengthened, stacked, (((left_axis,), (right_axis,)), ((), ())), preferred_element_type=f32
    )
    if len(right) == 1:
        return found
    return found[:, :wide] + found[:, wide:]


def indices():
    rows = lax.broadcasted_iota(jnp.int32, (CHUNK, CHUNK), 0)
    columns = lax.broadcasted_iota(jnp.int32, (CHUNK, CHUNK), 1)
    return rows, columns


def strength_of(packed):
    sources, half, lanes = packed.shape
    packed = packed.astype(f32)
    first = jnp.broadcast_to(packed[:, :, 0:1], (sources, half, lanes))
    second = jnp.broadcast_to(packed[:, :, lanes // 2 : lanes // 2 + 1], (sources, half, lanes))
    return jnp.concatenate([first, second], axis=1).reshape(sources * 2 * half, lanes)


def rows_of(ref, piece, start, count):
    sources = CHUNK // 32
    block = ref[piece * sources : (piece + 1) * sources, start : start + count, :]
    return block


def chunk_of(ref, piece, start):
    return rows_of(ref, piece, start, 32).reshape(CHUNK, ref.shape[2])


def key_terms(first_ref, piece, causal_ones):
    key = chunk_of(first_ref, piece, 0).astype(f32)
    decay = chunk_of(first_ref, piece, 32)
    weight = strength_of(rows_of(first_ref, piece, 64, 16))
    gamma = jnp.dot(causal_ones, decay, preferred_element_type=f32)
    middle = gamma[CHUNK // 2 - 1 : CHUNK // 2]
    last = gamma[CHUNK - 1 : CHUNK]
    inverse = lax.rsqrt(jnp.sum(key * key, axis=1, keepdims=True) + epsilon)
    unit = key * inverse
    rise = jnp.exp(gamma - middle)
    fall = jnp.exp(middle - gamma)
    head = jnp.exp(gamma)
    tail = jnp.exp(last - gamma)
    return dict(
        unit=unit, inverse=inverse, weight=weight, rise=rise, fall=fall, head=head, tail=tail, fade=jnp.exp(last)
    )


def spread_kernel(heads, first, second, third, *rest):
    *strength, out_ref = rest
    span = first.shape[0]
    for head in range(heads):
        lanes = slice(head * 128, (head + 1) * 128)
        out_ref[head, 0:span, :] = first[:, lanes]
        out_ref[head, span : 2 * span, :] = second[:, lanes]
        if third is not None:
            out_ref[head, 2 * span : 3 * span, :] = third[:, lanes]
    if strength:
        values = strength[0][...].astype(f32)
        half = span // 2
        early = lax.broadcasted_iota(jnp.int32, (half, 128), 1) < 64
        for head in range(heads):
            column = values[:, head : head + 1]
            packed = jnp.where(early, column[:half], column[half:])
            out_ref[head, 2 * span : 2 * span + half, :] = packed.astype(bf16)


def spread_keys(key_in, log_decay, strength):
    heads = strength.shape[1]

    def body(key_ref, decay_ref, strength_ref, out_ref):
        spread_kernel(heads, key_ref, decay_ref, None, strength_ref, out_ref)

    return pl.pallas_call(
        body, out_shape=jax.ShapeDtypeStruct((heads, 80, 128), bf16), compiler_params=params(), name="spread_keys"
    )(key_in, log_decay, strength)


def spread_values(values_in, queries, d_out, heads):
    def body(value_ref, query_ref, grad_ref, out_ref):
        spread_kernel(heads, value_ref, query_ref, grad_ref, out_ref)

    return pl.pallas_call(
        body, out_shape=jax.ShapeDtypeStruct((heads, 96, 128), bf16), compiler_params=params(), name="spread_values"
    )(values_in, queries, d_out)


def tree_levels(count):
    nodes = list(range(count))
    following = count
    found = []
    while len(nodes) > 1:
        above = []
        for left, right in zip(nodes[0::2], nodes[1::2]):
            found.append((following, left, right))
            above.append(following)
            following += 1
        nodes = above
    return found


def keys_kernel(pieces, first_ref, solve_ref, inner_ref, wkey_ref, transfer_ref):
    rows, columns = indices()
    causal_ones = jnp.where(rows >= columns, 1.0, 0.0).astype(bf16)
    strict = rows > columns
    eye = jnp.where(rows == columns, 1.0, 0.0)
    terms = [key_terms(first_ref, piece, causal_ones) for piece in range(pieces)]
    systems = []
    solved = []
    for piece in range(pieces):
        t = terms[piece]
        inner = product(parts(t["unit"] * t["rise"]), parts(t["unit"] * t["fall"]), 1, 1)
        inner = jnp.where(strict, inner, 0.0)
        inner_ref[piece] = inner
        system = t["weight"] * inner
        systems.append(system)
        pair = ((rows ^ columns) == 1) & strict
        solved.append(eye - jnp.where(pair, system, 0.0))
    shift = 1
    while (1 << shift) < CHUNK:
        row_block = lax.shift_right_logical(rows, shift)
        column_block = lax.shift_right_logical(columns, shift)
        corner = (row_block == column_block + 1) & ((row_block & 1) == 1)
        for piece in range(pieces):
            inverse = parts(solved[piece])
            block = parts(jnp.where(corner, systems[piece], 0.0))
            between = product(parts(product(inverse, block)), inverse)
            solved[piece] = solved[piece] - between
        shift += 1
    for piece in range(pieces):
        t = terms[piece]
        solve_ref[piece] = solved[piece]
        weighted = parts(t["weight"] * (t["unit"] * t["head"]))
        wkey = product(parts(solved[piece]), weighted)
        wkey_ref[piece] = wkey
        tail = parts(t["unit"] * t["tail"])
        transfer_ref[piece] = eye * t["fade"] - product(tail, parts(wkey), 0, 0)
    for parent, left, right in tree_levels(pieces):
        transfer_ref[parent] = product(parts(transfer_ref[right]), parts(transfer_ref[left]))


def keys_stage(first):
    pieces = first.shape[0] * 32 // CHUNK
    square = jax.ShapeDtypeStruct((pieces, CHUNK, CHUNK), f32)
    tree = jax.ShapeDtypeStruct((2 * pieces - 1, CHUNK, CHUNK), f32)

    def body(*refs):
        keys_kernel(pieces, *refs)

    return pl.pallas_call(
        body, out_shape=(square, square, square, tree), compiler_params=params(), name="keys_stage"
    )(first)


def query_terms(second_ref, piece):
    query = chunk_of(second_ref, piece, 32).astype(f32)
    inverse = lax.rsqrt(jnp.sum(query * query, axis=1, keepdims=True) + epsilon)
    return query * inverse, inverse


def values_kernel(
    pieces, first_ref, second_ref, solve_ref, wkey_ref, transfer_ref, wvalue_ref, scores_ref, offset_ref, inject_ref
):
    rows, columns = indices()
    causal_ones = jnp.where(rows >= columns, 1.0, 0.0).astype(bf16)
    causal = rows >= columns
    scale = CHUNK ** (-0.5)
    for piece in range(pieces):
        t = key_terms(first_ref, piece, causal_ones)
        query = query_terms(second_ref, piece)[0] * scale
        scores = product(parts(query * t["rise"]), parts(t["unit"] * t["fall"]), 1, 1)
        scores = jnp.where(causal, scores, 0.0)
        scores_ref[piece] = scores
        value = chunk_of(second_ref, piece, 0).astype(f32)
        wvalue = product(parts(solve_ref[piece]), parts(t["weight"] * value))
        wvalue_ref[piece] = wvalue
        offset_ref[piece] = product(parts(t["unit"] * t["tail"]), parts(wvalue), 0, 0)
        reach = query * t["head"] - product(parts(scores), parts(wkey_ref[piece]))
        grad = chunk_of(second_ref, piece, 64)
        inject_ref[piece] = product(parts(reach), (grad,), 0, 0)
    for parent, left, right in tree_levels(pieces):
        offset_ref[parent] = (
            product(parts(transfer_ref[right]), parts(offset_ref[left])) + offset_ref[right]
        )
        inject_ref[parent] = inject_ref[left] + product(
            parts(transfer_ref[left]), parts(inject_ref[right]), 0, 0
        )


def values_stage(first, second, solve, wkey, transfer):
    pieces = first.shape[0] * 32 // CHUNK
    square = jax.ShapeDtypeStruct((pieces, CHUNK, CHUNK), f32)
    tree = jax.ShapeDtypeStruct((2 * pieces - 1, CHUNK, CHUNK), f32)

    def body(*refs):
        values_kernel(pieces, *refs)

    return pl.pallas_call(
        body, out_shape=(square, square, tree, tree), compiler_params=params(), name="values_stage"
    )(first, second, solve, wkey, transfer)


def grads_kernel(
    pieces,
    blocks,
    place_ref,
    first_ref,
    second_ref,
    solve_ref,
    inner_ref,
    wkey_ref,
    transfer_ref,
    wvalue_ref,
    scores_ref,
    offset_ref,
    inject_ref,
    far_transfer_ref,
    far_ref,
    out_ref,
    state_ref,
    cot_ref,
):
    rows, columns = indices()
    causal = rows >= columns
    strict = rows > columns
    causal_ones = jnp.where(causal, 1.0, 0.0).astype(bf16)
    reverse_ones = jnp.where(rows <= columns, 1.0, 0.0).astype(bf16)
    sum_ones = jnp.ones((16, CHUNK), bf16)
    early = lax.broadcasted_iota(jnp.int32, (CHUNK // 32, 16, CHUNK), 2) < CHUNK // 2
    scale = CHUNK ** (-0.5)
    place = place_ref[0]
    state = jnp.where(place > 0, far_ref[0], 0.0)
    cot = jnp.where(place < blocks - 1, far_ref[blocks - 1], 0.0)
    for step in range(1, blocks - 1):
        back = blocks - 1 - step
        moved = product(parts(far_transfer_ref[step]), parts(state)) + far_ref[step]
        returned = product(parts(far_transfer_ref[back]), parts(cot), 0, 0) + far_ref[back]
        state = jnp.where(place > step, moved, state)
        cot = jnp.where(place < back, returned, cot)
    state_ref[2 * pieces - 2] = state
    cot_ref[2 * pieces - 2] = cot
    for parent, left, right in reversed(tree_levels(pieces)):
        state = state_ref[parent]
        cot = cot_ref[parent]
        state_ref[left] = state
        state_ref[right] = product(parts(transfer_ref[left]), parts(state)) + offset_ref[left]
        cot_ref[right] = cot
        cot_ref[left] = product(parts(transfer_ref[right]), parts(cot), 0, 0) + inject_ref[right]
    for piece in range(pieces):
        t = key_terms(first_ref, piece, causal_ones)
        query_one, query_inverse = query_terms(second_ref, piece)
        query = query_one * scale
        value = chunk_of(second_ref, piece, 0).astype(f32)
        grad = chunk_of(second_ref, piece, 64)
        state = state_ref[piece]
        cot = cot_ref[piece]
        state_parts = parts(state)
        cot_parts = parts(cot)
        unit = t["unit"]
        key_rise = unit * t["rise"]
        key_fall = unit * t["fall"]
        key_head = unit * t["head"]
        key_tail = unit * t["tail"]
        update = wvalue_ref[piece] - product(parts(wkey_ref[piece]), state_parts)
        update_parts = parts(update)
        d_update = product(parts(scores_ref[piece]), (grad,), 0, 0) + product(parts(key_tail), cot_parts)
        d_right = product(parts(solve_ref[piece]), parts(d_update), 0, 0)
        d_value = t["weight"] * d_right
        missed = value - product(parts(key_head), state_parts)
        missed = missed - product(parts(inner_ref[piece]), update_parts)
        d_weight = jnp.sum(d_right * missed, axis=1, keepdims=True)
        d_value_parts = parts(d_value)
        wide = CHUNK
        d_query_head = product((grad,), state_parts, 1, 1)
        d_key_head = -product(d_value_parts, state_parts, 1, 1)
        d_key_tail = product(update_parts, cot_parts, 1, 1)
        d_scores = jnp.where(causal, product((grad,), update_parts, 1, 1), 0.0)
        d_inner = jnp.where(strict, -product(d_value_parts, update_parts, 1, 1), 0.0)
        d_scores_parts = parts(d_scores)
        d_inner_parts = parts(d_inner)
        fall_parts = parts(key_fall)
        query_rise = query * t["rise"]
        d_query_rise = product(d_scores_parts, fall_parts)
        d_key_rise = product(d_inner_parts, fall_parts)
        d_key_fall = product(d_scores_parts, parts(query_rise), 0, 0) + product(
            d_inner_parts, parts(key_rise), 0, 0
        )
        d_query_unit = d_query_rise * t["rise"] + d_query_head * t["head"]
        up = d_key_rise * t["rise"] + d_key_head * t["head"]
        tail_term = d_key_tail * t["tail"]
        down = d_key_fall * t["fall"] + tail_term
        d_key_unit = up + down
        d_gamma = query * d_query_unit + unit * (up - down)
        faded = cot * state
        faded_high, faded_low = parts(faded)
        faded_rest = (faded - faded_high.astype(f32) - faded_low.astype(f32)).astype(bf16)
        d_fade = product((sum_ones,), (faded_high, faded_low), 1, 1) + product(
            (sum_ones,), (faded_rest,), 1, 1
        )
        d_last = jnp.sum(unit * tail_term, axis=0, keepdims=True) + d_fade[0:1] * t["fade"]
        gamma_high, gamma_low = parts(d_gamma)
        gamma_rest = (d_gamma - gamma_high.astype(f32) - gamma_low.astype(f32)).astype(bf16)
        d_decay = (
            product((reverse_ones,), (gamma_high, gamma_low))
            + product((reverse_ones,), (gamma_rest,))
            + d_last
        )
        d_query = (scale * query_inverse) * (
            d_query_unit - query_one * jnp.sum(query_one * d_query_unit, axis=1, keepdims=True)
        )
        d_key = t["inverse"] * (d_key_unit - unit * jnp.sum(unit * d_key_unit, axis=1, keepdims=True))
        sources = CHUNK // 32
        span = slice(piece * sources, (piece + 1) * sources)

        def shaped(array):
            return array.astype(bf16).reshape(sources, 32, wide)

        out_ref[span, 0:32, :] = shaped(d_query)
        out_ref[span, 32:64, :] = shaped(d_key)
        out_ref[span, 64:96, :] = shaped(d_value)
        out_ref[span, 96:128, :] = shaped(d_decay)
        weights = jnp.broadcast_to(d_weight, (CHUNK, CHUNK)).reshape(sources, 32, CHUNK)
        out_ref[span, 128:144, :] = jnp.where(early, weights[:, :16], weights[:, 16:]).astype(bf16)


def grads_stage(place, blocks, *arrays):
    first = arrays[0]
    sources = first.shape[0]
    pieces = sources * 32 // CHUNK

    def body(*refs):
        grads_kernel(pieces, blocks, *refs)

    return pl.pallas_call(
        body,
        in_specs=[pl.BlockSpec(memory_space=pltpu.SMEM)] + [pl.BlockSpec(memory_space=pltpu.VMEM)] * len(arrays),
        out_specs=pl.BlockSpec(memory_space=pltpu.VMEM),
        out_shape=jax.ShapeDtypeStruct((sources, 144, CHUNK), bf16),
        scratch_shapes=[pltpu.VMEM((2 * pieces - 1, CHUNK, CHUNK), f32)] * 2,
        compiler_params=params(),
        name="grads_stage",
    )(place, *arrays)


def unspread_kernel(packed_ref, query_ref, key_ref, value_ref, strength_ref, decay_ref):
    heads = packed_ref.shape[0]
    span = query_ref.shape[0]
    for head in range(heads):
        lanes = slice(head * 128, (head + 1) * 128)
        query_ref[:, lanes] = packed_ref[head, 0:span, :]
        key_ref[:, lanes] = packed_ref[head, span : 2 * span, :]
        value_ref[:, lanes] = packed_ref[head, 2 * span : 3 * span, :]
        decay_ref[:, lanes] = packed_ref[head, 3 * span : 4 * span, :]
    place = lax.broadcasted_iota(jnp.int32, (span, 128), 1)
    total = jnp.zeros((span, 128), f32)
    for head in range(heads):
        column = strength_of(packed_ref[head : head + 1, 4 * span : 4 * span + span // 2, :])
        total = jnp.where(place == head, column, total)
    strength_ref[...] = total[:, :heads].astype(bf16)


def unspread(packed, span):
    heads = packed.shape[0]
    wide = jax.ShapeDtypeStruct((span, heads * 128), bf16)
    return pl.pallas_call(
        unspread_kernel,
        out_shape=(wide, wide, wide, jax.ShapeDtypeStruct((span, heads), bf16), wide),
        compiler_params=params(),
        name="unspread",
    )(packed)


def per_device(queries, key_in, values_in, strength, log_decay, d_out):
    heads = strength.shape[1]
    blocks = lax.axis_size("block")
    place = lax.axis_index("block")

    def swap(array):
        return lax.all_to_all(array, ("near", "head"), 0, 0, tiled=True)

    def share(array):
        return lax.all_to_all(array, "block", 0, 0, tiled=True)

    first = swap(spread_keys(key_in, log_decay, strength))
    second = swap(spread_values(values_in, queries, d_out, heads))
    solve, inner, wkey, transfer = keys_stage(first)
    whole = (blocks, CHUNK, CHUNK)
    far_transfer = share(jnp.broadcast_to(transfer[-1], whole))
    wvalue, scores, offset, inject = values_stage(first, second, solve, wkey, transfer)
    later = lax.broadcasted_iota(jnp.int32, whole, 0) > place
    far = share(jnp.where(later, offset[-1], inject[-1]))
    packed = grads_stage(
        place.astype(jnp.int32).reshape(1),
        blocks,
        first,
        second,
        solve,
        inner,
        wkey,
        transfer,
        wvalue,
        scores,
        offset,
        inject,
        far_transfer,
        far,
    )
    return unspread(swap(packed), queries.shape[0])


def solution(mesh):
    heads_axis = mesh.shape["head"]
    near = 32 // heads_axis
    wide = Mesh(mesh.devices.reshape(-1, near, heads_axis), ("block", "near", "head"))
    spec = P(("block", "near", "head"), None)
    return jax.shard_map(
        per_device, mesh=wide, in_specs=(spec,) * 6, out_specs=(spec,) * 5, check_vma=False
    )
```

```python
import jax
import jax.numpy as jnp
from jax import lax
from jax.experimental import pallas as pl
from jax.experimental.pallas import tpu as pltpu
from jax.sharding import Mesh, PartitionSpec as P

epsilon = 1e-06
bf16 = jnp.bfloat16
f32 = jnp.float32
CHUNK = 128
VMEM_BYTES = 32 << 20


def params(size=VMEM_BYTES):
    return pltpu.CompilerParams(vmem_limit_bytes=size)


def parts(value):
    high = value.astype(bf16)
    return (high, (value - high.astype(f32)).astype(bf16))


def beside(arrays, axis):
    return arrays[0] if len(arrays) == 1 else jnp.concatenate(arrays, axis)


def product(left, right, left_axis=1, right_axis=0):
    wide = right[0].shape[1 - right_axis]
    row = beside(right, 1 - right_axis)
    stacked = beside([row] * len(left), right_axis)
    lengthened = beside(left, left_axis)
    found = lax.dot_general(
        lengthened, stacked, (((left_axis,), (right_axis,)), ((), ())), preferred_element_type=f32
    )
    if len(right) == 1:
        return found
    return found[:, :wide] + found[:, wide:]


def indices():
    rows = lax.broadcasted_iota(jnp.int32, (CHUNK, CHUNK), 0)
    columns = lax.broadcasted_iota(jnp.int32, (CHUNK, CHUNK), 1)
    return rows, columns


def strength_of(packed):
    sources, half, lanes = packed.shape
    packed = packed.astype(f32)
    first = jnp.broadcast_to(packed[:, :, 0:1], (sources, half, lanes))
    second = jnp.broadcast_to(packed[:, :, lanes // 2 : lanes // 2 + 1], (sources, half, lanes))
    return jnp.concatenate([first, second], axis=1).reshape(sources * 2 * half, lanes)


def tree_levels(count):
    nodes = list(range(count))
    following = count
    found = []
    while len(nodes) > 1:
        above = []
        for left, right in zip(nodes[0::2], nodes[1::2]):
            found.append((following, left, right))
            above.append(following)
            following += 1
        nodes = above
    return found


GROUP = 8
SPAN = 32
SOURCES = CHUNK // SPAN


def rows_of(ref, piece, start, count):
    return ref[piece * SOURCES : (piece + 1) * SOURCES, start : start + count, :]


def chunk_of(ref, piece, place):
    return rows_of(ref, piece, place * SPAN, SPAN).reshape(CHUNK, ref.shape[2])


def key_terms(packed_ref, piece, causal_ones):
    key = chunk_of(packed_ref, piece, 0).astype(f32)
    decay = chunk_of(packed_ref, piece, 1)
    weight = strength_of(rows_of(packed_ref, piece, 5 * SPAN, SPAN // 2))
    gamma = jnp.dot(causal_ones, decay, preferred_element_type=f32)
    middle = gamma[CHUNK // 2 - 1 : CHUNK // 2]
    last = gamma[CHUNK - 1 : CHUNK]
    inverse = lax.rsqrt(jnp.sum(key * key, axis=1, keepdims=True) + epsilon)
    unit = key * inverse
    rise = jnp.exp(gamma - middle)
    fall = jnp.exp(middle - gamma)
    head = jnp.exp(gamma)
    tail = jnp.exp(last - gamma)
    return dict(
        unit=unit, inverse=inverse, weight=weight, rise=rise, fall=fall, head=head, tail=tail, fade=jnp.exp(last)
    )


def query_terms(packed_ref, piece):
    query = chunk_of(packed_ref, piece, 3).astype(f32)
    inverse = lax.rsqrt(jnp.sum(query * query, axis=1, keepdims=True) + epsilon)
    return query * inverse, inverse


def spread_kernel(key_ref, decay_ref, value_ref, query_ref, grad_ref, strength_ref, out_ref):
    for head in range(GROUP):
        lanes = slice(head * 128, (head + 1) * 128)
        for place, ref in enumerate((key_ref, decay_ref, value_ref, query_ref, grad_ref)):
            out_ref[head, place * SPAN : (place + 1) * SPAN, :] = ref[:, lanes]
    values = strength_ref[...].astype(f32)
    heads = lax.broadcasted_iota(jnp.int32, values.shape, 1)
    half = SPAN // 2
    early = lax.broadcasted_iota(jnp.int32, (half, 128), 1) < 64
    for head in range(GROUP):
        chosen = heads == pl.program_id(0) * GROUP + head
        column = jnp.sum(jnp.where(chosen, values, 0.0), axis=1, keepdims=True)
        packed = jnp.where(early, column[:half], column[half:])
        out_ref[head, 5 * SPAN : 5 * SPAN + half, :] = packed.astype(bf16)


def spread(key_in, log_decay, values_in, queries, d_out, strength):
    span, heads = strength.shape
    rows = 5 * SPAN + SPAN // 2
    wide = pl.BlockSpec((span, GROUP * 128), lambda step: (0, step))
    return pl.pallas_call(
        spread_kernel,
        grid=(heads // GROUP,),
        in_specs=[wide] * 5 + [pl.BlockSpec((span, heads), lambda step: (0, 0))],
        out_specs=pl.BlockSpec((GROUP, rows, 128), lambda step: (step, 0, 0)),
        out_shape=jax.ShapeDtypeStruct((heads, rows, 128), bf16),
        compiler_params=params(58 << 20),
        name="spread",
    )(key_in, log_decay, values_in, queries, d_out, strength)


def joined(value):
    return jnp.concatenate(parts(value), axis=1)


def halves(value):
    return (value[:, :CHUNK], value[:, CHUNK:])


SOLVE, INNER, WKEY, SCORES = range(4)


def local_kernel(
    pieces, blocks, place_ref, packed_ref, share_ref, maps_ref, wvalue_ref, transfer_ref, left_ref, right_ref
):
    rows, columns = indices()
    causal = rows >= columns
    causal_ones = jnp.where(causal, 1.0, 0.0).astype(bf16)
    strict = rows > columns
    eye = jnp.where(rows == columns, 1.0, 0.0)
    scale = CHUNK ** (-0.5)
    terms = [key_terms(packed_ref, piece, causal_ones) for piece in range(pieces)]
    systems = []
    solved = []
    pair = ((rows ^ columns) == 1) & strict
    for piece in range(pieces):
        t = terms[piece]
        fall_parts = parts(t["unit"] * t["fall"])
        inner = product(parts(t["unit"] * t["rise"]), fall_parts, 1, 1)
        inner = jnp.where(strict, inner, 0.0)
        maps_ref[INNER, piece] = joined(inner)
        query = query_terms(packed_ref, piece)[0] * (scale * t["rise"])
        scores = jnp.where(causal, product(parts(query), fall_parts, 1, 1), 0.0)
        maps_ref[SCORES, piece] = joined(scores)
        system = t["weight"] * inner
        systems.append(system)
        solved.append(eye - jnp.where(pair, system, 0.0))
    shift = 1
    while (1 << shift) < CHUNK:
        row_block = lax.shift_right_logical(rows, shift)
        column_block = lax.shift_right_logical(columns, shift)
        corner = (row_block == column_block + 1) & ((row_block & 1) == 1)
        for piece in range(pieces):
            inverse = parts(solved[piece])
            block = parts(jnp.where(corner, systems[piece], 0.0))
            between = product(parts(product(inverse, block)), inverse)
            solved[piece] = solved[piece] - between
        shift += 1
    transfers = []
    offsets = []
    injects = []
    for piece in range(pieces):
        t = terms[piece]
        solve = parts(solved[piece])
        maps_ref[SOLVE, piece] = jnp.concatenate(solve, axis=1)
        value = chunk_of(packed_ref, piece, 2).astype(f32)
        wkey = parts(product(solve, parts(t["weight"] * (t["unit"] * t["head"]))))
        maps_ref[WKEY, piece] = jnp.concatenate(wkey, axis=1)
        wvalue = product(solve, parts(t["weight"] * value))
        wvalue_ref[piece] = wvalue
        tail = parts(t["unit"] * t["tail"])
        transfers.append(eye * t["fade"] - product(tail, wkey, 0, 0))
        offsets.append(product(tail, parts(wvalue), 0, 0))
        query = query_terms(packed_ref, piece)[0] * (scale * t["head"])
        reach = query - product(halves(maps_ref[SCORES, piece]), wkey)
        injects.append(product(parts(reach), (chunk_of(packed_ref, piece, 4),), 0, 0))
    for parent, left, right in tree_levels(pieces):
        transfer_left = parts(transfers[left])
        transfer_right = parts(transfers[right])
        transfer_ref[left] = jnp.concatenate(transfer_left, axis=1)
        transfer_ref[right] = jnp.concatenate(transfer_right, axis=1)
        left_ref[parent - pieces] = offsets[left]
        right_ref[parent - pieces] = injects[right]
        transfers.append(product(transfer_right, transfer_left))
        offsets.append(product(transfer_right, parts(offsets[left])) + offsets[right])
        injects.append(injects[left] + product(transfer_left, parts(injects[right]), 0, 0))
    place = place_ref[0]
    for block in range(blocks):
        share_ref[block, :CHUNK] = transfers[-1]
        share_ref[block, CHUNK:] = jnp.where(block > place, offsets[-1], injects[-1])


def saved_shapes(pieces):
    return (
        ((4, pieces, CHUNK, 2 * CHUNK), bf16),
        ((pieces, CHUNK, CHUNK), f32),
        ((2 * pieces - 2, CHUNK, 2 * CHUNK), bf16),
        ((pieces - 1, CHUNK, CHUNK), f32),
        ((pieces - 1, CHUNK, CHUNK), f32),
    )


def local_stage(place, blocks, packed):
    pieces = packed.shape[0] * SPAN // CHUNK
    saved = saved_shapes(pieces)

    def body(*refs):
        local_kernel(pieces, blocks, *refs)

    share, *found = pl.pallas_call(
        body,
        in_specs=[pl.BlockSpec(memory_space=pltpu.SMEM), pl.BlockSpec(memory_space=pltpu.VMEM)],
        out_shape=[jax.ShapeDtypeStruct((blocks, 2 * CHUNK, CHUNK), f32)]
        + [jax.ShapeDtypeStruct(shape, dtype) for shape, dtype in saved],
        compiler_params=params(),
        name="local_stage",
    )(place, packed)
    return share, found


def grads_kernel(
    pieces,
    blocks,
    place_ref,
    packed_ref,
    far_ref,
    maps_ref,
    wvalue_ref,
    transfer_ref,
    left_ref,
    right_ref,
    out_ref,
    state_ref,
    cot_ref,
):
    rows, columns = indices()
    causal = rows >= columns
    strict = rows > columns
    causal_ones = jnp.where(causal, 1.0, 0.0).astype(bf16)
    reverse_ones = jnp.where(rows <= columns, 1.0, 0.0).astype(bf16)
    sum_ones = jnp.ones((16, CHUNK), bf16)
    early = lax.broadcasted_iota(jnp.int32, (SOURCES, SPAN // 2, CHUNK), 2) < CHUNK // 2
    scale = CHUNK ** (-0.5)
    place = place_ref[0]
    state = jnp.where(place > 0, far_ref[0, CHUNK:], 0.0)
    cot = jnp.where(place < blocks - 1, far_ref[blocks - 1, CHUNK:], 0.0)
    for step in range(1, blocks - 1):
        back = blocks - 1 - step
        moved = product(parts(far_ref[step, :CHUNK]), parts(state)) + far_ref[step, CHUNK:]
        returned = product(parts(far_ref[back, :CHUNK]), parts(cot), 0, 0) + far_ref[back, CHUNK:]
        state = jnp.where(place > step, moved, state)
        cot = jnp.where(place < back, returned, cot)
    state_ref[2 * pieces - 2] = state
    cot_ref[2 * pieces - 2] = cot
    for parent, left, right in reversed(tree_levels(pieces)):
        state = state_ref[parent]
        cot = cot_ref[parent]
        state_ref[left] = state
        state_ref[right] = product(halves(transfer_ref[left]), parts(state)) + left_ref[parent - pieces]
        cot_ref[right] = cot
        cot_ref[left] = product(halves(transfer_ref[right]), parts(cot), 0, 0) + right_ref[parent - pieces]
    for piece in range(pieces):
        t = key_terms(packed_ref, piece, causal_ones)
        query_one, query_inverse = query_terms(packed_ref, piece)
        query = query_one * scale
        value = chunk_of(packed_ref, piece, 2).astype(f32)
        grad = chunk_of(packed_ref, piece, 4)
        state = state_ref[piece]
        cot = cot_ref[piece]
        state_parts = parts(state)
        cot_parts = parts(cot)
        unit = t["unit"]
        key_rise = unit * t["rise"]
        key_fall = unit * t["fall"]
        key_head = unit * t["head"]
        key_tail = unit * t["tail"]
        update = wvalue_ref[piece] - product(halves(maps_ref[WKEY, piece]), state_parts)
        update_parts = parts(update)
        d_update = product(halves(maps_ref[SCORES, piece]), (grad,), 0, 0) + product(parts(key_tail), cot_parts)
        d_right = product(halves(maps_ref[SOLVE, piece]), parts(d_update), 0, 0)
        d_value = t["weight"] * d_right
        missed = value - product(parts(key_head), state_parts)
        missed = missed - product(halves(maps_ref[INNER, piece]), update_parts)
        d_weight = jnp.sum(d_right * missed, axis=1, keepdims=True)
        d_value_parts = parts(d_value)
        d_query_head = product((grad,), state_parts, 1, 1)
        d_key_head = -product(d_value_parts, state_parts, 1, 1)
        d_key_tail = product(update_parts, cot_parts, 1, 1)
        d_scores = jnp.where(causal, product((grad,), update_parts, 1, 1), 0.0)
        d_inner = jnp.where(strict, -product(d_value_parts, update_parts, 1, 1), 0.0)
        d_scores_parts = parts(d_scores)
        d_inner_parts = parts(d_inner)
        fall_parts = parts(key_fall)
        query_rise = query * t["rise"]
        d_query_rise = product(d_scores_parts, fall_parts)
        d_key_rise = product(d_inner_parts, fall_parts)
        d_key_fall = product(d_scores_parts, parts(query_rise), 0, 0) + product(
            d_inner_parts, parts(key_rise), 0, 0
        )
        d_query_unit = d_query_rise * t["rise"] + d_query_head * t["head"]
        up = d_key_rise * t["rise"] + d_key_head * t["head"]
        tail_term = d_key_tail * t["tail"]
        down = d_key_fall * t["fall"] + tail_term
        d_key_unit = up + down
        d_gamma = query * d_query_unit + unit * (up - down)
        faded = cot * state
        faded_high, faded_low = parts(faded)
        faded_rest = (faded - faded_high.astype(f32) - faded_low.astype(f32)).astype(bf16)
        d_fade = product((sum_ones,), (faded_high, faded_low), 1, 1) + product(
            (sum_ones,), (faded_rest,), 1, 1
        )
        d_last = jnp.sum(unit * tail_term, axis=0, keepdims=True) + d_fade[0:1] * t["fade"]
        gamma_high, gamma_low = parts(d_gamma)
        gamma_rest = (d_gamma - gamma_high.astype(f32) - gamma_low.astype(f32)).astype(bf16)
        d_decay = (
            product((reverse_ones,), (gamma_high, gamma_low))
            + product((reverse_ones,), (gamma_rest,))
            + d_last
        )
        d_query = (scale * query_inverse) * (
            d_query_unit - query_one * jnp.sum(query_one * d_query_unit, axis=1, keepdims=True)
        )
        d_key = t["inverse"] * (d_key_unit - unit * jnp.sum(unit * d_key_unit, axis=1, keepdims=True))
        span = slice(piece * SOURCES, (piece + 1) * SOURCES)

        def shaped(array):
            return array.astype(bf16).reshape(SOURCES, SPAN, CHUNK)

        out_ref[span, 0:32, :] = shaped(d_query)
        out_ref[span, 32:64, :] = shaped(d_key)
        out_ref[span, 64:96, :] = shaped(d_value)
        out_ref[span, 96:128, :] = shaped(d_decay)
        weights = jnp.broadcast_to(d_weight, (CHUNK, CHUNK)).reshape(SOURCES, SPAN, CHUNK)
        out_ref[span, 128:144, :] = jnp.where(early, weights[:, :16], weights[:, 16:]).astype(bf16)


def grads_stage(place, packed, far, saved):
    sources = packed.shape[0]
    pieces = sources * SPAN // CHUNK
    blocks = far.shape[0]

    def body(*refs):
        grads_kernel(pieces, blocks, *refs)

    return pl.pallas_call(
        body,
        in_specs=[pl.BlockSpec(memory_space=pltpu.SMEM)]
        + [pl.BlockSpec(memory_space=pltpu.VMEM)] * (2 + len(saved)),
        out_specs=pl.BlockSpec(memory_space=pltpu.VMEM),
        out_shape=jax.ShapeDtypeStruct((sources, 4 * SPAN + SPAN // 2, CHUNK), bf16),
        scratch_shapes=[pltpu.VMEM((2 * pieces - 1, CHUNK, CHUNK), f32)] * 2,
        compiler_params=params(),
        name="grads_stage",
    )(place, packed, far, *saved)


def unspread_kernel(packed_ref, query_ref, key_ref, value_ref, decay_ref, strength_ref):
    for head in range(GROUP):
        lanes = slice(head * 128, (head + 1) * 128)
        for place, ref in enumerate((query_ref, key_ref, value_ref, decay_ref)):
            ref[:, lanes] = packed_ref[head, place * SPAN : (place + 1) * SPAN, :]
    first = pl.program_id(0) * GROUP
    place = lax.broadcasted_iota(jnp.int32, (SPAN, 128), 1)
    total = jnp.zeros((SPAN, 128), f32)
    for head in range(GROUP):
        column = strength_of(packed_ref[head : head + 1, 4 * SPAN : 4 * SPAN + SPAN // 2, :])
        total = jnp.where(place == first + head, column, total)
    chosen = (place >= first) & (place < first + GROUP)
    heads = strength_ref.shape[1]
    before = strength_ref[...].astype(f32)
    strength_ref[...] = jnp.where(chosen[:, :heads], total[:, :heads], before).astype(bf16)


def unspread(packed, span):
    heads, rows, _ = packed.shape
    wide = jax.ShapeDtypeStruct((span, heads * 128), bf16)
    spec = pl.BlockSpec((span, GROUP * 128), lambda step: (0, step))
    return pl.pallas_call(
        unspread_kernel,
        grid=(heads // GROUP,),
        in_specs=[pl.BlockSpec((GROUP, rows, 128), lambda step: (step, 0, 0))],
        out_specs=(spec, spec, spec, spec, pl.BlockSpec((span, heads), lambda step: (0, 0))),
        out_shape=(wide, wide, wide, wide, jax.ShapeDtypeStruct((span, heads), bf16)),
        compiler_params=params(),
        name="unspread",
    )(packed)


def per_device(queries, key_in, values_in, strength, log_decay, d_out):
    blocks = lax.axis_size("block")
    place = lax.axis_index("block").astype(jnp.int32).reshape(1)

    def swap(array):
        return lax.all_to_all(array, ("near", "head"), 0, 0, tiled=True)

    packed = swap(spread(key_in, log_decay, values_in, queries, d_out, strength))
    share, saved = local_stage(place, blocks, packed)
    far = lax.all_to_all(share, "block", 0, 0, tiled=True)
    d_packed = swap(grads_stage(place, packed, far, saved))
    d_query, d_key, d_value, d_decay, d_strength = unspread(d_packed, queries.shape[0])
    return d_query, d_key, d_value, d_strength, d_decay


def solution(mesh):
    heads_axis = mesh.shape["head"]
    near = 32 // heads_axis
    wide = Mesh(mesh.devices.reshape(-1, near, heads_axis), ("block", "near", "head"))
    spec = P(("block", "near", "head"), None)
    return jax.shard_map(
        per_device, mesh=wide, in_specs=(spec,) * 6, out_specs=(spec,) * 5, check_vma=False
    )
```

```python
import jax
import jax.numpy as jnp
from jax import lax
from jax.experimental import pallas as pl
from jax.experimental.pallas import tpu as pltpu
from jax.sharding import Mesh, PartitionSpec as P

epsilon = 1e-06
bf16 = jnp.bfloat16
f32 = jnp.float32
CHUNK = 128
VMEM_BYTES = 32 << 20


def params(size=VMEM_BYTES):
    return pltpu.CompilerParams(vmem_limit_bytes=size)


def parts(value):
    high = value.astype(bf16)
    return (high, (value - high.astype(f32)).astype(bf16))


def beside(arrays, axis):
    return arrays[0] if len(arrays) == 1 else jnp.concatenate(arrays, axis)


def product(left, right, left_axis=1, right_axis=0):
    wide = right[0].shape[1 - right_axis]
    row = beside(right, 1 - right_axis)
    stacked = beside([row] * len(left), right_axis)
    lengthened = beside(left, left_axis)
    found = lax.dot_general(
        lengthened, stacked, (((left_axis,), (right_axis,)), ((), ())), preferred_element_type=f32
    )
    if len(right) == 1:
        return found
    return found[:, :wide] + found[:, wide:]


def indices():
    rows = lax.broadcasted_iota(jnp.int32, (CHUNK, CHUNK), 0)
    columns = lax.broadcasted_iota(jnp.int32, (CHUNK, CHUNK), 1)
    return rows, columns


def strength_of(packed):
    sources, rows, lanes = packed.shape
    packed = packed.astype(f32)
    found = []
    for place in range(FOLD):
        lane = place * (lanes // FOLD)
        found.append(jnp.broadcast_to(packed[:, :, lane : lane + 1], (sources, rows, lanes)))
    return jnp.concatenate(found, axis=1).reshape(sources * FOLD * rows, lanes)


def strength_folded(values):
    sources, rows, _ = values.shape
    rows = rows // FOLD
    lane = lax.broadcasted_iota(jnp.int32, (sources, rows, 128), 2)
    found = jnp.broadcast_to(values[:, :rows], (sources, rows, 128))
    for place in range(1, FOLD):
        found = jnp.where(lane >= place * (128 // FOLD), values[:, place * rows : (place + 1) * rows], found)
    return found.astype(bf16)


def in_step(bodies):
    bodies = list(bodies)
    while bodies:
        running = []
        for body in bodies:
            if next(body, True) is None:
                running.append(body)
        bodies = running


def tree_levels(count):
    nodes = list(range(count))
    following = count
    found = []
    while len(nodes) > 1:
        above = []
        for left, right in zip(nodes[0::2], nodes[1::2]):
            found.append((following, left, right))
            above.append(following)
            following += 1
        nodes = above
    return found


GROUP = 16
FOLD = 4
SPAN = 32
SOURCES = CHUNK // SPAN


def rows_of(ref, piece, start, count):
    return ref[piece * SOURCES : (piece + 1) * SOURCES, start : start + count, :]


def chunk_of(ref, piece, place):
    return rows_of(ref, piece, place * SPAN, SPAN).reshape(CHUNK, ref.shape[2])


def key_terms(packed_ref, piece, causal_ones):
    key = chunk_of(packed_ref, piece, 0).astype(f32)
    decay = chunk_of(packed_ref, piece, 1)
    weight = strength_of(rows_of(packed_ref, piece, 5 * SPAN, SPAN // FOLD))
    gamma = jnp.dot(causal_ones, decay, preferred_element_type=f32)
    middle = gamma[CHUNK // 2 - 1 : CHUNK // 2]
    last = gamma[CHUNK - 1 : CHUNK]
    inverse = lax.rsqrt(jnp.sum(key * key, axis=1, keepdims=True) + epsilon)
    unit = key * inverse
    rise = jnp.exp(gamma - middle)
    fall = jnp.exp(middle - gamma)
    head = jnp.exp(gamma)
    tail = jnp.exp(last - gamma)
    return dict(
        unit=unit, inverse=inverse, weight=weight, rise=rise, fall=fall, head=head, tail=tail, fade=jnp.exp(last)
    )


def query_terms(packed_ref, piece):
    query = chunk_of(packed_ref, piece, 3).astype(f32)
    inverse = lax.rsqrt(jnp.sum(query * query, axis=1, keepdims=True) + epsilon)
    return query * inverse, inverse


def spread_kernel(key_ref, decay_ref, value_ref, query_ref, grad_ref, strength_ref, out_ref):
    for head in range(GROUP):
        lanes = slice(head * 128, (head + 1) * 128)
        for place, ref in enumerate((key_ref, decay_ref, value_ref, query_ref, grad_ref)):
            out_ref[head, place * SPAN : (place + 1) * SPAN, :] = ref[:, lanes]
    values = strength_ref[...].astype(f32)
    heads = lax.broadcasted_iota(jnp.int32, values.shape, 1)
    for head in range(GROUP):
        chosen = heads == pl.program_id(0) * GROUP + head
        column = jnp.sum(jnp.where(chosen, values, 0.0), axis=1, keepdims=True)
        out_ref[head : head + 1, 5 * SPAN :, :] = strength_folded(column[None])


def spread(key_in, log_decay, values_in, queries, d_out, strength):
    span, heads = strength.shape
    rows = 5 * SPAN + SPAN // FOLD
    wide = pl.BlockSpec((span, GROUP * 128), lambda step: (0, step))
    return pl.pallas_call(
        spread_kernel,
        grid=(heads // GROUP,),
        in_specs=[wide] * 5 + [pl.BlockSpec((span, heads), lambda step: (0, 0))],
        out_specs=pl.BlockSpec((GROUP, rows, 128), lambda step: (step, 0, 0)),
        out_shape=jax.ShapeDtypeStruct((heads, rows, 128), bf16),
        compiler_params=params(58 << 20),
        name="spread",
    )(key_in, log_decay, values_in, queries, d_out, strength)


def joined(value):
    return jnp.concatenate(parts(value), axis=1)


def halves(value):
    return (value[:, :CHUNK], value[:, CHUNK:])


SOLVE, INNER, WKEY, SCORES = range(4)


def local_kernel(
    pieces, blocks, place_ref, packed_ref, share_ref, maps_ref, wvalue_ref, transfer_ref, left_ref, right_ref
):
    rows, columns = indices()
    causal = rows >= columns
    causal_ones = jnp.where(causal, 1.0, 0.0).astype(bf16)
    strict = rows > columns
    eye = jnp.where(rows == columns, 1.0, 0.0)
    scale = CHUNK ** (-0.5)
    terms = [None] * pieces
    systems = [None] * pieces
    solved = [None] * pieces
    pair = ((rows ^ columns) == 1) & strict

    def begin(piece):
        t = terms[piece] = key_terms(packed_ref, piece, causal_ones)
        query = query_terms(packed_ref, piece)[0] * scale
        yield
        fall_parts = parts(t["unit"] * t["fall"])
        inner = product(parts(t["unit"] * t["rise"]), fall_parts, 1, 1)
        yield
        scores = product(parts(query * t["rise"]), fall_parts, 1, 1)
        yield
        inner = jnp.where(strict, inner, 0.0)
        maps_ref[INNER, piece] = joined(inner)
        systems[piece] = t["weight"] * inner
        solved[piece] = eye - jnp.where(pair, systems[piece], 0.0)
        yield
        maps_ref[SCORES, piece] = joined(jnp.where(causal, scores, 0.0))

    in_step(begin(piece) for piece in range(pieces))
    shift = 1
    while (1 << shift) < CHUNK:
        row_block = lax.shift_right_logical(rows, shift)
        column_block = lax.shift_right_logical(columns, shift)
        corner = (row_block == column_block + 1) & ((row_block & 1) == 1)

        def widen(piece):
            inverse = parts(solved[piece])
            between = product(inverse, parts(jnp.where(corner, systems[piece], 0.0)))
            yield
            solved[piece] = solved[piece] - product(parts(between), inverse)

        in_step(widen(piece) for piece in range(pieces))
        shift += 1
    transfers = [None] * pieces
    offsets = [None] * pieces
    injects = [None] * pieces

    def end(piece):
        t = terms[piece]
        solve = parts(solved[piece])
        maps_ref[SOLVE, piece] = jnp.concatenate(solve, axis=1)
        wkey = parts(product(solve, parts(t["weight"] * (t["unit"] * t["head"]))))
        yield
        maps_ref[WKEY, piece] = jnp.concatenate(wkey, axis=1)
        wvalue = product(solve, parts(t["weight"] * chunk_of(packed_ref, piece, 2).astype(f32)))
        yield
        wvalue_ref[piece] = wvalue
        tail = parts(t["unit"] * t["tail"])
        transfers[piece] = eye * t["fade"] - product(tail, wkey, 0, 0)
        yield
        offsets[piece] = product(tail, parts(wvalue), 0, 0)
        yield
        query = query_terms(packed_ref, piece)[0] * (scale * t["head"])
        reach = query - product(halves(maps_ref[SCORES, piece]), wkey)
        yield
        injects[piece] = product(parts(reach), (chunk_of(packed_ref, piece, 4),), 0, 0)

    in_step(end(piece) for piece in range(pieces))
    for parent, left, right in tree_levels(pieces):
        transfer_left = parts(transfers[left])
        transfer_right = parts(transfers[right])
        transfer_ref[left] = jnp.concatenate(transfer_left, axis=1)
        transfer_ref[right] = jnp.concatenate(transfer_right, axis=1)
        left_ref[parent - pieces] = offsets[left]
        right_ref[parent - pieces] = injects[right]
        transfers.append(product(transfer_right, transfer_left))
        offsets.append(product(transfer_right, parts(offsets[left])) + offsets[right])
        injects.append(injects[left] + product(transfer_left, parts(injects[right]), 0, 0))
    place = place_ref[0]
    for block in range(blocks):
        share_ref[block, :CHUNK] = transfers[-1]
        share_ref[block, CHUNK:] = jnp.where(block > place, offsets[-1], injects[-1])


def saved_shapes(pieces):
    return (
        ((4, pieces, CHUNK, 2 * CHUNK), bf16),
        ((pieces, CHUNK, CHUNK), f32),
        ((2 * pieces - 2, CHUNK, 2 * CHUNK), bf16),
        ((pieces - 1, CHUNK, CHUNK), f32),
        ((pieces - 1, CHUNK, CHUNK), f32),
    )


def local_stage(place, blocks, packed):
    pieces = packed.shape[0] * SPAN // CHUNK
    saved = saved_shapes(pieces)

    def body(*refs):
        local_kernel(pieces, blocks, *refs)

    share, *found = pl.pallas_call(
        body,
        in_specs=[pl.BlockSpec(memory_space=pltpu.SMEM), pl.BlockSpec(memory_space=pltpu.VMEM)],
        out_shape=[jax.ShapeDtypeStruct((blocks, 2 * CHUNK, CHUNK), f32)]
        + [jax.ShapeDtypeStruct(shape, dtype) for shape, dtype in saved],
        compiler_params=params(),
        name="local_stage",
    )(place, packed)
    return share, found


def grads_kernel(
    pieces,
    blocks,
    place_ref,
    packed_ref,
    far_ref,
    maps_ref,
    wvalue_ref,
    transfer_ref,
    left_ref,
    right_ref,
    out_ref,
    state_ref,
    cot_ref,
):
    rows, columns = indices()
    causal = rows >= columns
    strict = rows > columns
    causal_ones = jnp.where(causal, 1.0, 0.0).astype(bf16)
    reverse_ones = jnp.where(rows <= columns, 1.0, 0.0).astype(bf16)
    sum_ones = jnp.ones((16, CHUNK), bf16)
    scale = CHUNK ** (-0.5)
    place = place_ref[0]
    state = jnp.where(place > 0, far_ref[0, CHUNK:], 0.0)
    cot = jnp.where(place < blocks - 1, far_ref[blocks - 1, CHUNK:], 0.0)
    for step in range(1, blocks - 1):
        back = blocks - 1 - step
        moved = product(parts(far_ref[step, :CHUNK]), parts(state)) + far_ref[step, CHUNK:]
        returned = product(parts(far_ref[back, :CHUNK]), parts(cot), 0, 0) + far_ref[back, CHUNK:]
        state = jnp.where(place > step, moved, state)
        cot = jnp.where(place < back, returned, cot)
    state_ref[2 * pieces - 2] = state
    cot_ref[2 * pieces - 2] = cot
    for parent, left, right in reversed(tree_levels(pieces)):
        state = state_ref[parent]
        cot = cot_ref[parent]
        state_ref[left] = state
        state_ref[right] = product(halves(transfer_ref[left]), parts(state)) + left_ref[parent - pieces]
        cot_ref[right] = cot
        cot_ref[left] = product(halves(transfer_ref[right]), parts(cot), 0, 0) + right_ref[parent - pieces]
    def work(piece):
        t = key_terms(packed_ref, piece, causal_ones)
        query_one, query_inverse = query_terms(packed_ref, piece)
        query = query_one * scale
        value = chunk_of(packed_ref, piece, 2).astype(f32)
        grad = chunk_of(packed_ref, piece, 4)
        yield
        state = state_ref[piece]
        cot = cot_ref[piece]
        state_parts = parts(state)
        cot_parts = parts(cot)
        unit = t["unit"]
        key_rise = unit * t["rise"]
        key_fall = unit * t["fall"]
        key_head = unit * t["head"]
        key_tail = unit * t["tail"]
        update = wvalue_ref[piece] - product(halves(maps_ref[WKEY, piece]), state_parts)
        yield
        update_parts = parts(update)
        d_update = product(halves(maps_ref[SCORES, piece]), (grad,), 0, 0) + product(parts(key_tail), cot_parts)
        yield
        d_right = product(halves(maps_ref[SOLVE, piece]), parts(d_update), 0, 0)
        d_value = t["weight"] * d_right
        missed = value - product(parts(key_head), state_parts)
        yield
        missed = missed - product(halves(maps_ref[INNER, piece]), update_parts)
        d_weight = jnp.sum(d_right * missed, axis=1, keepdims=True)
        d_value_parts = parts(d_value)
        d_query_head = product((grad,), state_parts, 1, 1)
        yield
        d_key_head = -product(d_value_parts, state_parts, 1, 1)
        d_key_tail = product(update_parts, cot_parts, 1, 1)
        d_scores = jnp.where(causal, product((grad,), update_parts, 1, 1), 0.0)
        d_inner = jnp.where(strict, -product(d_value_parts, update_parts, 1, 1), 0.0)
        yield
        d_scores_parts = parts(d_scores)
        d_inner_parts = parts(d_inner)
        fall_parts = parts(key_fall)
        query_rise = query * t["rise"]
        d_query_rise = product(d_scores_parts, fall_parts)
        d_key_rise = product(d_inner_parts, fall_parts)
        yield
        d_key_fall = product(d_scores_parts, parts(query_rise), 0, 0) + product(
            d_inner_parts, parts(key_rise), 0, 0
        )
        yield
        d_query_unit = d_query_rise * t["rise"] + d_query_head * t["head"]
        up = d_key_rise * t["rise"] + d_key_head * t["head"]
        tail_term = d_key_tail * t["tail"]
        down = d_key_fall * t["fall"] + tail_term
        d_key_unit = up + down
        d_gamma = query * d_query_unit + unit * (up - down)
        faded = cot * state
        faded_high, faded_low = parts(faded)
        faded_rest = (faded - faded_high.astype(f32) - faded_low.astype(f32)).astype(bf16)
        yield
        d_fade = product((sum_ones,), (faded_high, faded_low), 1, 1) + product(
            (sum_ones,), (faded_rest,), 1, 1
        )
        d_last = jnp.sum(unit * tail_term, axis=0, keepdims=True) + d_fade[0:1] * t["fade"]
        gamma_high, gamma_low = parts(d_gamma)
        gamma_rest = (d_gamma - gamma_high.astype(f32) - gamma_low.astype(f32)).astype(bf16)
        yield
        d_decay = (
            product((reverse_ones,), (gamma_high, gamma_low))
            + product((reverse_ones,), (gamma_rest,))
            + d_last
        )
        yield
        d_query = (scale * query_inverse) * (
            d_query_unit - query_one * jnp.sum(query_one * d_query_unit, axis=1, keepdims=True)
        )
        d_key = t["inverse"] * (d_key_unit - unit * jnp.sum(unit * d_key_unit, axis=1, keepdims=True))
        span = slice(piece * SOURCES, (piece + 1) * SOURCES)

        def shaped(array):
            return array.astype(bf16).reshape(SOURCES, SPAN, CHUNK)

        out_ref[span, 0:32, :] = shaped(d_query)
        out_ref[span, 32:64, :] = shaped(d_key)
        out_ref[span, 64:96, :] = shaped(d_value)
        out_ref[span, 96:128, :] = shaped(d_decay)
        weights = jnp.broadcast_to(d_weight, (CHUNK, CHUNK)).reshape(SOURCES, SPAN, CHUNK)
        out_ref[span, 4 * SPAN :, :] = strength_folded(weights)

    in_step(work(piece) for piece in range(pieces))


def grads_stage(place, packed, far, saved):
    sources = packed.shape[0]
    pieces = sources * SPAN // CHUNK
    blocks = far.shape[0]

    def body(*refs):
        grads_kernel(pieces, blocks, *refs)

    return pl.pallas_call(
        body,
        in_specs=[pl.BlockSpec(memory_space=pltpu.SMEM)]
        + [pl.BlockSpec(memory_space=pltpu.VMEM)] * (2 + len(saved)),
        out_specs=pl.BlockSpec(memory_space=pltpu.VMEM),
        out_shape=jax.ShapeDtypeStruct((sources, 4 * SPAN + SPAN // FOLD, CHUNK), bf16),
        scratch_shapes=[pltpu.VMEM((2 * pieces - 1, CHUNK, CHUNK), f32)] * 2,
        compiler_params=params(),
        name="grads_stage",
    )(place, packed, far, *saved)


def unspread_kernel(packed_ref, query_ref, key_ref, value_ref, decay_ref, strength_ref):
    for head in range(GROUP):
        lanes = slice(head * 128, (head + 1) * 128)
        for place, ref in enumerate((query_ref, key_ref, value_ref, decay_ref)):
            ref[:, lanes] = packed_ref[head, place * SPAN : (place + 1) * SPAN, :]
    first = pl.program_id(0) * GROUP
    place = lax.broadcasted_iota(jnp.int32, (SPAN, 128), 1)
    total = jnp.zeros((SPAN, 128), f32)
    for head in range(GROUP):
        column = strength_of(packed_ref[head : head + 1, 4 * SPAN :, :])
        total = jnp.where(place == first + head, column, total)
    chosen = (place >= first) & (place < first + GROUP)
    heads = strength_ref.shape[1]
    before = strength_ref[...].astype(f32)
    strength_ref[...] = jnp.where(chosen[:, :heads], total[:, :heads], before).astype(bf16)


def unspread(packed, span):
    heads, rows, _ = packed.shape
    wide = jax.ShapeDtypeStruct((span, heads * 128), bf16)
    spec = pl.BlockSpec((span, GROUP * 128), lambda step: (0, step))
    return pl.pallas_call(
        unspread_kernel,
        grid=(heads // GROUP,),
        in_specs=[pl.BlockSpec((GROUP, rows, 128), lambda step: (step, 0, 0))],
        out_specs=(spec, spec, spec, spec, pl.BlockSpec((span, heads), lambda step: (0, 0))),
        out_shape=(wide, wide, wide, wide, jax.ShapeDtypeStruct((span, heads), bf16)),
        compiler_params=params(),
        name="unspread",
    )(packed)


def per_device(queries, key_in, values_in, strength, log_decay, d_out):
    blocks = lax.axis_size("block")
    place = lax.axis_index("block").astype(jnp.int32).reshape(1)

    def swap(array):
        return lax.all_to_all(array, ("near", "head"), 0, 0, tiled=True)

    packed = swap(spread(key_in, log_decay, values_in, queries, d_out, strength))
    share, saved = local_stage(place, blocks, packed)
    far = lax.all_to_all(share, "block", 0, 0, tiled=True)
    d_packed = swap(grads_stage(place, packed, far, saved))
    d_query, d_key, d_value, d_decay, d_strength = unspread(d_packed, queries.shape[0])
    return d_query, d_key, d_value, d_strength, d_decay


def solution(mesh):
    heads_axis = mesh.shape["head"]
    near = 32 // heads_axis
    wide = Mesh(mesh.devices.reshape(-1, near, heads_axis), ("block", "near", "head"))
    spec = P(("block", "near", "head"), None)
    return jax.shard_map(
        per_device, mesh=wide, in_specs=(spec,) * 6, out_specs=(spec,) * 5, check_vma=False
    )
```

```python
import jax
import jax.numpy as jnp
from jax import lax
from jax.experimental import pallas as pl
from jax.experimental.pallas import tpu as pltpu
from jax.sharding import Mesh, PartitionSpec as P

epsilon = 1e-06
bf16 = jnp.bfloat16
f32 = jnp.float32
CHUNK = 128
VMEM_BYTES = 32 << 20


def params(size=VMEM_BYTES):
    return pltpu.CompilerParams(vmem_limit_bytes=size)


def parts(value):
    high = value.astype(bf16)
    return (high, (value - high.astype(f32)).astype(bf16))


def beside(arrays, axis):
    return arrays[0] if len(arrays) == 1 else jnp.concatenate(arrays, axis)


def product(left, right, left_axis=1, right_axis=0):
    wide = right[0].shape[1 - right_axis]
    row = beside(right, 1 - right_axis)
    stacked = beside([row] * len(left), right_axis)
    lengthened = beside(left, left_axis)
    found = lax.dot_general(
        lengthened, stacked, (((left_axis,), (right_axis,)), ((), ())), preferred_element_type=f32
    )
    if len(right) == 1:
        return found
    return found[:, :wide] + found[:, wide:]


def indices():
    rows = lax.broadcasted_iota(jnp.int32, (CHUNK, CHUNK), 0)
    columns = lax.broadcasted_iota(jnp.int32, (CHUNK, CHUNK), 1)
    return rows, columns


def strength_of(packed):
    sources, rows, lanes = packed.shape
    packed = packed.astype(f32)
    found = []
    for place in range(FOLD):
        lane = place * (lanes // FOLD)
        found.append(jnp.broadcast_to(packed[:, :, lane : lane + 1], (sources, rows, lanes)))
    return jnp.concatenate(found, axis=1).reshape(sources * FOLD * rows, lanes)


def strength_folded(values):
    sources, rows, _ = values.shape
    rows = rows // FOLD
    lane = lax.broadcasted_iota(jnp.int32, (sources, rows, 128), 2)
    found = jnp.broadcast_to(values[:, :rows], (sources, rows, 128))
    for place in range(1, FOLD):
        found = jnp.where(lane >= place * (128 // FOLD), values[:, place * rows : (place + 1) * rows], found)
    return found.astype(bf16)


def in_step(bodies):
    bodies = list(bodies)
    while bodies:
        running = []
        for body in bodies:
            if next(body, True) is None:
                running.append(body)
        bodies = running


def tree_levels(count):
    nodes = list(range(count))
    following = count
    found = []
    while len(nodes) > 1:
        above = []
        for left, right in zip(nodes[0::2], nodes[1::2]):
            found.append((following, left, right))
            above.append(following)
            following += 1
        nodes = above
    return found


GROUP = 16
FOLD = 4
SPAN = 32
SOURCES = CHUNK // SPAN


def rows_of(ref, piece, start, count):
    return ref[piece * SOURCES : (piece + 1) * SOURCES, start : start + count, :]


def chunk_of(ref, piece, place):
    return rows_of(ref, piece, place * SPAN, SPAN).reshape(CHUNK, ref.shape[2])


def key_terms(packed_ref, piece, causal_ones):
    key = chunk_of(packed_ref, piece, 0).astype(f32)
    decay = chunk_of(packed_ref, piece, 1)
    weight = strength_of(rows_of(packed_ref, piece, 5 * SPAN, SPAN // FOLD))
    gamma = jnp.dot(causal_ones, decay, preferred_element_type=f32)
    middle = gamma[CHUNK // 2 - 1 : CHUNK // 2]
    last = gamma[CHUNK - 1 : CHUNK]
    inverse = lax.rsqrt(jnp.sum(key * key, axis=1, keepdims=True) + epsilon)
    unit = key * inverse
    rise = jnp.exp(gamma - middle)
    fall = jnp.exp(middle - gamma)
    head = jnp.exp(gamma)
    tail = jnp.exp(last - gamma)
    return dict(
        unit=unit, inverse=inverse, weight=weight, rise=rise, fall=fall, head=head, tail=tail, fade=jnp.exp(last)
    )


def query_terms(packed_ref, piece):
    query = chunk_of(packed_ref, piece, 3).astype(f32)
    inverse = lax.rsqrt(jnp.sum(query * query, axis=1, keepdims=True) + epsilon)
    return query * inverse, inverse


def spread_kernel(key_ref, decay_ref, value_ref, query_ref, grad_ref, strength_ref, out_ref):
    for head in range(GROUP):
        lanes = slice(head * 128, (head + 1) * 128)
        for place, ref in enumerate((key_ref, decay_ref, value_ref, query_ref, grad_ref)):
            out_ref[head, place * SPAN : (place + 1) * SPAN, :] = ref[:, lanes]
    values = strength_ref[...].astype(f32)
    heads = lax.broadcasted_iota(jnp.int32, values.shape, 1)
    for head in range(GROUP):
        chosen = heads == pl.program_id(0) * GROUP + head
        column = jnp.sum(jnp.where(chosen, values, 0.0), axis=1, keepdims=True)
        out_ref[head : head + 1, 5 * SPAN :, :] = strength_folded(column[None])


def spread(key_in, log_decay, values_in, queries, d_out, strength):
    span, heads = strength.shape
    rows = 5 * SPAN + SPAN // FOLD
    wide = pl.BlockSpec((span, GROUP * 128), lambda step: (0, step))
    return pl.pallas_call(
        spread_kernel,
        grid=(heads // GROUP,),
        in_specs=[wide] * 5 + [pl.BlockSpec((span, heads), lambda step: (0, 0))],
        out_specs=pl.BlockSpec((GROUP, rows, 128), lambda step: (step, 0, 0)),
        out_shape=jax.ShapeDtypeStruct((heads, rows, 128), bf16),
        compiler_params=params(58 << 20),
        name="spread",
    )(key_in, log_decay, values_in, queries, d_out, strength)


def joined(value):
    return jnp.concatenate(parts(value), axis=1)


def halves(value):
    return (value[:, :CHUNK], value[:, CHUNK:])


SOLVE, INNER, WKEY, SCORES = range(4)


def local_kernel(
    pieces, blocks, place_ref, packed_ref, share_ref, maps_ref, wvalue_ref, transfer_ref, left_ref, right_ref
):
    rows, columns = indices()
    causal = rows >= columns
    causal_ones = jnp.where(causal, 1.0, 0.0).astype(bf16)
    strict = rows > columns
    eye = jnp.where(rows == columns, 1.0, 0.0)
    scale = CHUNK ** (-0.5)
    terms = [None] * pieces
    systems = [None] * pieces
    solved = [None] * pieces
    pair = ((rows ^ columns) == 1) & strict

    def begin(piece):
        t = terms[piece] = key_terms(packed_ref, piece, causal_ones)
        query = query_terms(packed_ref, piece)[0] * scale
        yield
        fall_parts = parts(t["unit"] * t["fall"])
        inner = product(parts(t["unit"] * t["rise"]), fall_parts, 1, 1)
        yield
        scores = product(parts(query * t["rise"]), fall_parts, 1, 1)
        yield
        inner = jnp.where(strict, inner, 0.0)
        maps_ref[INNER, piece] = joined(inner)
        systems[piece] = t["weight"] * inner
        solved[piece] = eye - jnp.where(pair, systems[piece], 0.0)
        yield
        maps_ref[SCORES, piece] = joined(jnp.where(causal, scores, 0.0))

    in_step(begin(piece) for piece in range(pieces))
    shift = 1
    while (1 << shift) < CHUNK:
        row_block = lax.shift_right_logical(rows, shift)
        column_block = lax.shift_right_logical(columns, shift)
        corner = (row_block == column_block + 1) & ((row_block & 1) == 1)

        def widen(piece):
            inverse = parts(solved[piece])
            between = product(inverse, parts(jnp.where(corner, systems[piece], 0.0)))
            yield
            solved[piece] = solved[piece] - product(parts(between), inverse)

        in_step(widen(piece) for piece in range(pieces))
        shift += 1
    transfers = [None] * pieces
    offsets = [None] * pieces
    injects = [None] * pieces

    def end(piece):
        t = terms[piece]
        solve = parts(solved[piece])
        maps_ref[SOLVE, piece] = jnp.concatenate(solve, axis=1)
        wkey = parts(product(solve, parts(t["weight"] * (t["unit"] * t["head"]))))
        yield
        maps_ref[WKEY, piece] = jnp.concatenate(wkey, axis=1)
        wvalue = product(solve, parts(t["weight"] * chunk_of(packed_ref, piece, 2).astype(f32)))
        yield
        wvalue_ref[piece] = wvalue
        tail = parts(t["unit"] * t["tail"])
        transfers[piece] = eye * t["fade"] - product(tail, wkey, 0, 0)
        yield
        offsets[piece] = product(tail, parts(wvalue), 0, 0)
        yield
        query = query_terms(packed_ref, piece)[0] * (scale * t["head"])
        reach = query - product(halves(maps_ref[SCORES, piece]), wkey)
        yield
        injects[piece] = product(parts(reach), (chunk_of(packed_ref, piece, 4),), 0, 0)

    in_step(end(piece) for piece in range(pieces))
    for parent, left, right in tree_levels(pieces):
        transfer_left = parts(transfers[left])
        transfer_right = parts(transfers[right])
        transfer_ref[left] = jnp.concatenate(transfer_left, axis=1)
        transfer_ref[right] = jnp.concatenate(transfer_right, axis=1)
        left_ref[parent - pieces] = offsets[left]
        right_ref[parent - pieces] = injects[right]
        transfers.append(product(transfer_right, transfer_left))
        offsets.append(product(transfer_right, parts(offsets[left])) + offsets[right])
        injects.append(injects[left] + product(transfer_left, parts(injects[right]), 0, 0))
    place = place_ref[0]
    for block in range(blocks):
        share_ref[block, :CHUNK] = transfers[-1]
        share_ref[block, CHUNK:] = jnp.where(block > place, offsets[-1], injects[-1])


def saved_shapes(pieces):
    return (
        ((4, pieces, CHUNK, 2 * CHUNK), bf16),
        ((pieces, CHUNK, CHUNK), f32),
        ((2 * pieces - 2, CHUNK, 2 * CHUNK), bf16),
        ((pieces - 1, CHUNK, CHUNK), f32),
        ((pieces - 1, CHUNK, CHUNK), f32),
    )


def local_stage(place, blocks, packed):
    pieces = packed.shape[0] * SPAN // CHUNK
    saved = saved_shapes(pieces)

    def body(*refs):
        local_kernel(pieces, blocks, *refs)

    share, *found = pl.pallas_call(
        body,
        in_specs=[pl.BlockSpec(memory_space=pltpu.SMEM), pl.BlockSpec(memory_space=pltpu.VMEM)],
        out_shape=[jax.ShapeDtypeStruct((blocks, 2 * CHUNK, CHUNK), f32)]
        + [jax.ShapeDtypeStruct(shape, dtype) for shape, dtype in saved],
        compiler_params=params(),
        name="local_stage",
    )(place, packed)
    return share, found


def grads_kernel(
    pieces,
    blocks,
    place_ref,
    packed_ref,
    far_ref,
    maps_ref,
    wvalue_ref,
    transfer_ref,
    left_ref,
    right_ref,
    out_ref,
    state_ref,
    cot_ref,
):
    rows, columns = indices()
    causal = rows >= columns
    strict = rows > columns
    causal_ones = jnp.where(causal, 1.0, 0.0).astype(bf16)
    reverse_ones = jnp.where(rows <= columns, 1.0, 0.0).astype(bf16)
    sum_ones = jnp.ones((16, CHUNK), bf16)
    scale = CHUNK ** (-0.5)
    place = place_ref[0]
    ready = [None] * pieces

    def relay():
        state = jnp.where(place > 0, far_ref[0, CHUNK:], 0.0)
        cot = jnp.where(place < blocks - 1, far_ref[blocks - 1, CHUNK:], 0.0)
        for step in range(1, blocks - 1):
            back = blocks - 1 - step
            moved = product(parts(far_ref[step, :CHUNK]), parts(state)) + far_ref[step, CHUNK:]
            returned = product(parts(far_ref[back, :CHUNK]), parts(cot), 0, 0) + far_ref[back, CHUNK:]
            state = jnp.where(place > step, moved, state)
            cot = jnp.where(place < back, returned, cot)
            yield
        state_ref[2 * pieces - 2] = state
        cot_ref[2 * pieces - 2] = cot

    def prepare(piece):
        t = key_terms(packed_ref, piece, causal_ones)
        yield
        query_one, query_inverse = query_terms(packed_ref, piece)
        yield
        fall_parts = parts(t["unit"] * t["fall"])
        yield
        from_grad = product(halves(maps_ref[SCORES, piece]), (chunk_of(packed_ref, piece, 4),), 0, 0)
        yield
        ready[piece] = (t, query_one, query_inverse, fall_parts, from_grad)

    in_step([relay()] + [prepare(piece) for piece in range(pieces)])
    for parent, left, right in reversed(tree_levels(pieces)):
        state = state_ref[parent]
        cot = cot_ref[parent]
        state_ref[left] = state
        state_ref[right] = product(halves(transfer_ref[left]), parts(state)) + left_ref[parent - pieces]
        cot_ref[right] = cot
        cot_ref[left] = product(halves(transfer_ref[right]), parts(cot), 0, 0) + right_ref[parent - pieces]

    def work(piece):
        t, query_one, query_inverse, fall_parts, from_grad = ready[piece]
        query = query_one * scale
        value = chunk_of(packed_ref, piece, 2).astype(f32)
        grad = chunk_of(packed_ref, piece, 4)
        yield
        state = state_ref[piece]
        cot = cot_ref[piece]
        state_parts = parts(state)
        cot_parts = parts(cot)
        unit = t["unit"]
        key_rise = unit * t["rise"]
        key_head = unit * t["head"]
        key_tail = unit * t["tail"]
        update = wvalue_ref[piece] - product(halves(maps_ref[WKEY, piece]), state_parts)
        yield
        update_parts = parts(update)
        d_update = from_grad + product(parts(key_tail), cot_parts)
        yield
        d_right = product(halves(maps_ref[SOLVE, piece]), parts(d_update), 0, 0)
        d_value = t["weight"] * d_right
        missed = value - product(parts(key_head), state_parts)
        yield
        missed = missed - product(halves(maps_ref[INNER, piece]), update_parts)
        d_weight = jnp.sum(d_right * missed, axis=1, keepdims=True)
        d_value_parts = parts(d_value)
        d_query_head = product((grad,), state_parts, 1, 1)
        yield
        d_key_head = -product(d_value_parts, state_parts, 1, 1)
        d_key_tail = product(update_parts, cot_parts, 1, 1)
        d_scores = jnp.where(causal, product((grad,), update_parts, 1, 1), 0.0)
        d_inner = jnp.where(strict, -product(d_value_parts, update_parts, 1, 1), 0.0)
        yield
        d_scores_parts = parts(d_scores)
        d_inner_parts = parts(d_inner)
        query_rise = query * t["rise"]
        d_query_rise = product(d_scores_parts, fall_parts)
        d_key_rise = product(d_inner_parts, fall_parts)
        yield
        d_key_fall = product(d_scores_parts, parts(query_rise), 0, 0) + product(
            d_inner_parts, parts(key_rise), 0, 0
        )
        yield
        d_query_unit = d_query_rise * t["rise"] + d_query_head * t["head"]
        up = d_key_rise * t["rise"] + d_key_head * t["head"]
        tail_term = d_key_tail * t["tail"]
        down = d_key_fall * t["fall"] + tail_term
        d_key_unit = up + down
        d_gamma = query * d_query_unit + unit * (up - down)
        faded = cot * state
        faded_high, faded_low = parts(faded)
        faded_rest = (faded - faded_high.astype(f32) - faded_low.astype(f32)).astype(bf16)
        yield
        d_fade = product((sum_ones,), (faded_high, faded_low), 1, 1) + product(
            (sum_ones,), (faded_rest,), 1, 1
        )
        d_last = jnp.sum(unit * tail_term, axis=0, keepdims=True) + d_fade[0:1] * t["fade"]
        gamma_high, gamma_low = parts(d_gamma)
        gamma_rest = (d_gamma - gamma_high.astype(f32) - gamma_low.astype(f32)).astype(bf16)
        yield
        d_decay = (
            product((reverse_ones,), (gamma_high, gamma_low))
            + product((reverse_ones,), (gamma_rest,))
            + d_last
        )
        yield
        d_query = (scale * query_inverse) * (
            d_query_unit - query_one * jnp.sum(query_one * d_query_unit, axis=1, keepdims=True)
        )
        d_key = t["inverse"] * (d_key_unit - unit * jnp.sum(unit * d_key_unit, axis=1, keepdims=True))
        span = slice(piece * SOURCES, (piece + 1) * SOURCES)

        def shaped(array):
            return array.astype(bf16).reshape(SOURCES, SPAN, CHUNK)

        out_ref[span, 0:32, :] = shaped(d_query)
        out_ref[span, 32:64, :] = shaped(d_key)
        out_ref[span, 64:96, :] = shaped(d_value)
        out_ref[span, 96:128, :] = shaped(d_decay)
        weights = jnp.broadcast_to(d_weight, (CHUNK, CHUNK)).reshape(SOURCES, SPAN, CHUNK)
        out_ref[span, 4 * SPAN :, :] = strength_folded(weights)

    in_step(work(piece) for piece in range(pieces))


def grads_stage(place, packed, far, saved):
    sources = packed.shape[0]
    pieces = sources * SPAN // CHUNK
    blocks = far.shape[0]

    def body(*refs):
        grads_kernel(pieces, blocks, *refs)

    return pl.pallas_call(
        body,
        in_specs=[pl.BlockSpec(memory_space=pltpu.SMEM)]
        + [pl.BlockSpec(memory_space=pltpu.VMEM)] * (2 + len(saved)),
        out_specs=pl.BlockSpec(memory_space=pltpu.VMEM),
        out_shape=jax.ShapeDtypeStruct((sources, 4 * SPAN + SPAN // FOLD, CHUNK), bf16),
        scratch_shapes=[pltpu.VMEM((2 * pieces - 1, CHUNK, CHUNK), f32)] * 2,
        compiler_params=params(),
        name="grads_stage",
    )(place, packed, far, *saved)


def unspread_kernel(packed_ref, query_ref, key_ref, value_ref, decay_ref, strength_ref):
    for head in range(GROUP):
        lanes = slice(head * 128, (head + 1) * 128)
        for place, ref in enumerate((query_ref, key_ref, value_ref, decay_ref)):
            ref[:, lanes] = packed_ref[head, place * SPAN : (place + 1) * SPAN, :]
    first = pl.program_id(0) * GROUP
    place = lax.broadcasted_iota(jnp.int32, (SPAN, 128), 1)
    total = jnp.zeros((SPAN, 128), f32)
    for head in range(GROUP):
        column = strength_of(packed_ref[head : head + 1, 4 * SPAN :, :])
        total = jnp.where(place == first + head, column, total)
    chosen = (place >= first) & (place < first + GROUP)
    heads = strength_ref.shape[1]
    before = strength_ref[...].astype(f32)
    strength_ref[...] = jnp.where(chosen[:, :heads], total[:, :heads], before).astype(bf16)


def unspread(packed, span):
    heads, rows, _ = packed.shape
    wide = jax.ShapeDtypeStruct((span, heads * 128), bf16)
    spec = pl.BlockSpec((span, GROUP * 128), lambda step: (0, step))
    return pl.pallas_call(
        unspread_kernel,
        grid=(heads // GROUP,),
        in_specs=[pl.BlockSpec((GROUP, rows, 128), lambda step: (step, 0, 0))],
        out_specs=(spec, spec, spec, spec, pl.BlockSpec((span, heads), lambda step: (0, 0))),
        out_shape=(wide, wide, wide, wide, jax.ShapeDtypeStruct((span, heads), bf16)),
        compiler_params=params(),
        name="unspread",
    )(packed)


def per_device(queries, key_in, values_in, strength, log_decay, d_out):
    blocks = lax.axis_size("block")
    place = lax.axis_index("block").astype(jnp.int32).reshape(1)

    def swap(array):
        return lax.all_to_all(array, ("near", "head"), 0, 0, tiled=True)

    packed = swap(spread(key_in, log_decay, values_in, queries, d_out, strength))
    share, saved = local_stage(place, blocks, packed)
    far = lax.all_to_all(share, "block", 0, 0, tiled=True)
    d_packed = swap(grads_stage(place, packed, far, saved))
    d_query, d_key, d_value, d_decay, d_strength = unspread(d_packed, queries.shape[0])
    return d_query, d_key, d_value, d_strength, d_decay


def solution(mesh):
    heads_axis = mesh.shape["head"]
    near = 32 // heads_axis
    wide = Mesh(mesh.devices.reshape(-1, near, heads_axis), ("block", "near", "head"))
    spec = P(("block", "near", "head"), None)
    return jax.shard_map(
        per_device, mesh=wide, in_specs=(spec,) * 6, out_specs=(spec,) * 5, check_vma=False
    )
```
